32 devices in a mesh: groups: 2 (over x), tensor: 16 (over z, y, core).
Axes of the slice: x: 2, y: 2, z: 4, core: 2. Of those that a mesh axis runs over, the one named last changes fastest.
Arguments:
- tile_cols: int32 [16, 2], P('groups'), parts along dimension 0, may hold values from 0 to 7, as said below
- pair_list: int32 [8], P('groups'), parts along dimension 0, may hold values from 0 to 3, each once
- amplitudes: bfloat16 [8, 8, 2, 9216], P('groups', None, None, 'tensor'), parts along dimension 0, may hold values from -6 to 6
- factors: bfloat16 [2304, 16, 2, 9216], P('tensor', 'groups'), parts along dimension 1, may hold values from -0.09375 to 0.09375
Outputs:
- residual: float32 [8, 8, 2, 9216], P('groups', None, None, 'tensor'), parts along dimension 0
The draws below stay inside these ranges and needn't reach their ends.
There are 2 independent parts, one for each index of `groups`. The reference program is written for one: setup_inputs(seed, part) draws one part's arguments, and reference() takes and returns one part's arrays. A program takes and returns all parts, laid end to end along the dimension named above; each array names one. Nothing has to cross between parts.
Inputs may be any that keep to these rules, and one draw needn't show every extreme that they name: `tile_cols`: each row names 2 different tiles, the first being the row's own tile. `pair_list`: each stored pair once.
All inputs are finite; a program needn't handle non-finite values.
Results may differ from the reference program's by a relative error of at most 0.0028.
Values may be sent and summed in bfloat16 or wider, within the bound.
A program may use at most 256 MiB of HBM per device.

```python
import jax
import jax.numpy as jnp
from jax import lax

W = 96
NT = 8
KB = 2
NAUX = 2304
NPAIR = 4


def draw_tile_cols(key, part):
    key = jax.random.fold_in(key, 11)
    scores = jax.random.randint(key, (NT, NT), 0, 1 << 20)
    scores = scores * NT + jnp.arange(NT, dtype=jnp.int32)[None, :]
    scores = jnp.where(jnp.eye(NT, dtype=bool), -1, scores)
    ordering = jnp.argsort(scores, axis=1)
    return ordering[:, :KB].astype(jnp.int32)


def raised(array, own_key, source, target, blocks, factor):
    def block_of(dim):
        return (jnp.arange(array.shape[dim]) // (array.shape[dim] // blocks)).reshape((-1,) + (1,) * (array.ndim - 1 - dim))

    near = jax.random.permutation(own_key, blocks)[block_of(target)]
    far = (block_of(target) + blocks // 2) % blocks
    return jnp.where((block_of(source) == near) | (block_of(source) == far), factor * array, array)


def block_scale(stream_key, shape, shards, least, high):
    loudness, own = 1.0, jax.random.fold_in(stream_key, 6)
    for position, shards_of in shards:
        heights = jnp.exp(jax.random.uniform(jax.random.fold_in(own, position), (shards_of,), jnp.float32, least / len(shards), high / len(shards)))
        loudness = loudness * jnp.repeat(heights, shape[position] // shards_of).reshape([-1 if axis == position else 1 for axis in range(len(shape))])
    return loudness


def scatter_about(key, dims, scale, limit, shards=(), kind=jnp.bfloat16):
    gain = block_scale(key, dims, shards, -0.22, 0.18) if shards else 1.0
    drawn = jax.random.normal(key, dims, jnp.float32) * scale * gain
    return jnp.minimum(jnp.maximum(drawn, -limit), limit).astype(kind)


def heavy_noise(own_key, dims, deviation, reach, cuts, heavy, kind=jnp.bfloat16):
    array = deviation * jax.random.normal(own_key, dims, jnp.float32)
    if cuts:
        array = array * block_scale(own_key, dims, cuts, -0.22, 0.18)
    return jnp.clip(raised(array, jax.random.fold_in(own_key, 3), *heavy), -reach, reach).astype(kind)


def setup_inputs(seed: int = 0, part: int = 0) -> dict:
    arg_keys = jax.random.split(jax.random.key(seed), 5)
    own_keys = jax.random.split(jax.random.fold_in(arg_keys[4], part), 5)
    tile_cols = draw_tile_cols(jax.random.fold_in(jax.random.fold_in(arg_keys[4], part), 71), part)
    pair_list = jax.random.permutation(own_keys[1], NPAIR).astype(jnp.int32)
    amplitudes = scatter_about(own_keys[2], (NPAIR, NT, KB, W * W), 1.0, 6.0, ((3, 16),))
    factors = heavy_noise(own_keys[3], (NAUX, NT, KB, W * W), (KB * W * NAUX // 48) ** -0.5, 0.09375, ((0, 16),), (0, 3, 16, 2.0))
    return {"tile_cols": tile_cols, "pair_list": pair_list, "amplitudes": amplitudes, "factors": factors}


def reference(tile_cols, pair_list, amplitudes, factors):
    reached = tile_cols[tile_cols]
    matches = (reached[:, :, None, None, :] == reached[:, None, :, :, None]).astype(jnp.float32)
    chosen = amplitudes[pair_list].astype(jnp.float32).reshape(NPAIR, NT, KB, W, W)
    routed = chosen[:, tile_cols]
    picked = jnp.einsum('aikjm,saimvw->saikjvw', matches, routed, precision=lax.Precision.HIGHEST)
    blocked = factors.reshape(NAUX // 8, 8, NT, KB, W * W)

    def advance(total, aux_block):
        factor_tiles = aux_block.astype(jnp.float32).reshape(8, NT, KB, W, W)
        half_done = jnp.einsum('paiuv,saikjvw->spakjuw', factor_tiles, picked, precision=lax.Precision.HIGHEST)
        half_done = lax.optimization_barrier(half_done.astype(jnp.bfloat16)).astype(jnp.float32)
        partner = factor_tiles[:, tile_cols]
        update = jnp.einsum('spakjuw,pakjxw->sakux', half_done, partner, precision=lax.Precision.HIGHEST)
        return total + update, None

    start = jnp.zeros((NPAIR, NT, KB, W, W), jnp.float32)
    total, unused = lax.scan(advance, start, blocked)
    return total.reshape(NPAIR, NT, KB, W * W)
```

```python
import functools

import jax
import jax.numpy as jnp
from jax import lax
from jax.experimental import pallas as pl
from jax.experimental.pallas import tpu as pltpu
from jax.sharding import PartitionSpec as P

W = 96
NT = 8
KB = 2
LANES = 128
WIDE = KB * LANES
CHUNKS = W * W // LANES
GROUP = W // 4
HALVES = 2
VMEM = 56 * 1024 * 1024


def lay_kernel(block, x_ref, y_ref, flat_ref, tile_ref):
    lane = lax.broadcasted_iota(jnp.int32, (GROUP, LANES), 1)

    def one(p, carry):
        for a in range(NT):
            flat_ref[a] = x_ref[p, a].astype(jnp.float32)
            for k in range(KB):
                first, second, third = (
                    flat_ref[a, pl.ds(KB * j + k, GROUP, stride=3 * KB), :] for j in range(3)
                )
                rows = (
                    first,
                    pltpu.roll(jnp.where(lane >= 96, first, second), 32, 1),
                    pltpu.roll(jnp.where(lane >= 64, second, third), 64, 1),
                    pltpu.roll(third, 96, 1),
                )
                for r in range(4):
                    tile_ref[a, k, pl.ds(r, GROUP, stride=4), :] = jnp.where(lane < W, rows[r], 0.0)
            for k in range(KB):
                y_ref[p, a, :, k * LANES : (k + 1) * LANES] = tile_ref[a, k].astype(jnp.bfloat16)
        return carry

    lax.fori_loop(0, block, one, 0)


def lay(flat):
    count = flat.shape[0]
    block = max(c for c in (1, 2, 3, 4, 6, 8) if count % c == 0)
    chunked = flat.reshape(count, NT, KB, CHUNKS, LANES).transpose(0, 1, 3, 2, 4)
    chunked = chunked.reshape(count, NT, CHUNKS * KB, LANES)
    return pl.pallas_call(
        functools.partial(lay_kernel, block),
        grid=(count // block,),
        in_specs=[pl.BlockSpec((block, NT, CHUNKS * KB, LANES), lambda i: (i, 0, 0, 0))],
        out_specs=pl.BlockSpec((block, NT, W, WIDE), lambda i: (i, 0, 0, 0)),
        scratch_shapes=[
            pltpu.VMEM((NT, CHUNKS * KB, LANES), jnp.float32),
            pltpu.VMEM((NT, KB, W, LANES), jnp.float32),
        ],
        out_shape=jax.ShapeDtypeStruct((count, NT, W, WIDE), jnp.bfloat16),
        compiler_params=pltpu.CompilerParams(vmem_limit_bytes=VMEM),
        cost_estimate=pl.CostEstimate(
            flops=flat.size, bytes_accessed=flat.size * 5, transcendentals=0
        ),
    )(chunked)


def ladder_kernel(slots, block, first, count, near_ref, b_ref, tile_ref, out_ref, half_ref, t_ref):
    stride = 3 * LANES

    @pl.when(pl.program_id(0) == 0)
    def _():
        out_ref[...] = jnp.zeros_like(out_ref)
        t_ref[...] = jnp.zeros_like(t_ref)
        for i in range(count):
            near = near_ref[first + i]
            closed = near_ref[near] == first + i
            for s in range(slots):
                at = s * stride
                own = tile_ref[s, first + i]
                beside = tile_ref[s, near]
                t_ref[i, 0:W, at : at + WIDE] = own
                t_ref[i, LANES : LANES + W, at + LANES : at + LANES + WIDE] = beside

                @pl.when(closed)
                def _():
                    t_ref[i, 0:W, at + WIDE : at + stride] = tile_ref[s, first + i, :, 0:LANES]
                    t_ref[i, LANES : LANES + W, at : at + LANES] = tile_ref[s, near, :, LANES:WIDE]

    def form(i):
        for p in range(block):
            half = lax.dot_general(
                b_ref[p, first + i],
                t_ref[i],
                (((1,), (0,)), ((), ())),
                preferred_element_type=jnp.float32,
            ).astype(jnp.bfloat16)
            for s in range(slots):
                half_ref[i % 2, p, s * W : (s + 1) * W, :] = half[:, s * stride : (s + 1) * stride]

    def close(i):
        near = near_ref[first + i]
        for k, d in ((0, first + i), (1, near)):
            left = jnp.concatenate(
                [half_ref[i % 2, p, :, k * LANES : k * LANES + WIDE] for p in range(block)], axis=1
            )
            right = jnp.concatenate([b_ref[p, d] for p in range(block)], axis=1)
            part = lax.dot_general(
                left, right, (((1,), (1,)), ((), ())), preferred_element_type=jnp.float32
            )
            for s in range(slots):
                out_ref[s, i, k] += part[s * W : (s + 1) * W]

    for i in range(count):
        form(i)
        if i:
            close(i - 1)
    close(count - 1)


def ladder(near, rows, tiles, first, count):
    aux, slots = rows.shape[0], tiles.shape[0]
    block = max(c for c in (1, 2, 3, 4, 6, 8) if aux % c == 0)
    return pl.pallas_call(
        functools.partial(ladder_kernel, slots, block, first, count),
        grid_spec=pltpu.PrefetchScalarGridSpec(
            num_scalar_prefetch=1,
            grid=(aux // block,),
            in_specs=[
                pl.BlockSpec((block, NT, W, WIDE), lambda i, near: (i, 0, 0, 0)),
                pl.BlockSpec(memory_space=pltpu.VMEM),
            ],
            out_specs=pl.BlockSpec((slots, count, KB, W, W), lambda i, near: (0, 0, 0, 0, 0)),
            scratch_shapes=[
                pltpu.VMEM((2, block, slots * W, 3 * LANES), jnp.bfloat16),
                pltpu.VMEM((count, WIDE, slots * 3 * LANES), jnp.bfloat16),
            ],
        ),
        out_shape=jax.ShapeDtypeStruct((slots, count, KB, W, W), jnp.float32),
        compiler_params=pltpu.CompilerParams(vmem_limit_bytes=VMEM),
        cost_estimate=pl.CostEstimate(
            flops=aux * count * slots * 8 * 2 * W**3, bytes_accessed=rows.size * 2, transcendentals=0
        ),
    )(near, rows, tiles)


def settle(part, merged):
    size = lax.axis_size("tensor")
    slots, count = part.shape[:2]
    tile = (W * W,) if W % size else (W, W)
    lead = ((slots, count, KB), (slots, count * KB), (slots * count * KB,))[merged]
    share = lax.psum_scatter(
        part.reshape(lead + tile), "tensor", scatter_dimension=len(lead), tiled=True
    )
    return share.reshape(slots, count, KB, W * W // size)


def on_device(tile_cols, pair_list, amplitudes, factors):
    chosen = jnp.take(amplitudes, pair_list, axis=0)
    slots, share = chosen.shape[0], chosen.shape[3]
    pieces = lax.all_gather(chosen.reshape(slots * NT * KB, share), "tensor")
    tiles = lay(pieces.transpose(1, 0, 2).reshape(slots, NT, KB, W * W))
    rows = lay(factors)
    near = tile_cols[:, 1]
    count = NT // HALVES
    shares = [settle(ladder(near, rows, tiles, h * count, count), h) for h in range(HALVES)]
    return jnp.concatenate(shares, axis=1)


def solution(mesh):
    placed = (
        P("groups", None),
        P("groups"),
        P("groups", None, None, "tensor"),
        P("tensor", "groups", None, None),
    )
    return jax.shard_map(
        on_device,
        mesh=mesh,
        in_specs=placed,
        out_specs=P("groups", None, None, "tensor"),
        check_vma=False,
    )
```
